32 devices in a mesh: seq: 8 (over z, x), mp: 4 (over y, core).
Axes of the slice: x: 2, y: 2, z: 4, core: 2. Of those that a mesh axis runs over, the one named last changes fastest.
Arguments:
- fields_in: bfloat16 [2048, 3, 4096], P('seq', None, 'mp'), may hold values from -6 to 6
- pack_source: int32 [2048], P('seq'), may hold values from 0 to 2047, as said below
- doc_start: int32 [2048], P('seq'), may hold values from 0 to 2047, as said below
- short_filter: float32 [3, 3, 4096], P(None, None, 'mp'), may hold values from -2.4 to 2.4
- memory: float32 [2, 4096], P(None, 'mp'), may hold values from 30 to 8192
- residue: float32 [2, 4096], P(None, 'mp'), may hold values from -4 to 4
- skip_gain: float32 [4096], P('mp'), may hold values from -2.5 to 2.5
- w_out: bfloat16 [4096, 4096], P('mp'), may hold values from -0.09375 to 0.09375
- cotangent: bfloat16 [2048, 4096], P('seq', 'mp'), may hold values from -6 to 6
Outputs:
- mixed: bfloat16 [2048, 4096], P('seq', 'mp')
- d_fields: bfloat16 [2048, 3, 4096], P('seq', None, 'mp')
- d_filter: float32 [3, 3, 4096], P(None, None, 'mp')
- d_residue: float32 [2, 4096], P(None, 'mp')
- d_skip: float32 [4096], P('mp')
The draws below stay inside these ranges and needn't reach their ends.
Inputs may be any that keep to these rules, and one draw needn't show every extreme that they name: pack_source is a permutation of the 2048 loader rows. Of the 256 positions of one aligned block, at most 64 take rows of one and the same aligned block of loader rows, and in every draw some pair of blocks reaches 64. doc_start[t] is the first position of the document that holds position t; documents are runs of consecutive positions, and the longest has exactly 1024 positions.
All inputs are finite; a program needn't handle non-finite values.
Results may differ from the reference program's by a relative error of at most 0.0049.
Values may be sent and summed in bfloat16 or wider, within the bound.
A program may use at most 256 MiB of HBM per device.

```python
import jax
import jax.numpy as jnp
from jax import lax

D = 4096
TOK_DEV = 256
MODES = 2
TOKENS = 2048
MOST_DOC = 1024
N_SEQ = 8


def draw_pack_source(key, part):
    count = N_SEQ
    mean = TOK_DEV // count
    keys = jax.random.split(jax.random.fold_in(key, 11), 4)
    pairing = jax.random.permutation(keys[0], count)
    moved = jax.random.randint(keys[1], (count // 2,), 0, mean + 1).astype(jnp.int32).at[0].set(mean)
    share = jnp.full((count,), mean, jnp.int32).at[pairing[0::2]].add(moved).at[pairing[1::2]].add(-moved)
    offset = jax.random.permutation(keys[2], count)
    owners = jnp.arange(count, dtype=jnp.int32)
    counts = share[(owners[None, :] - offset[:, None]) % count]
    ends = jnp.cumsum(counts, axis=1)
    starts = ends - counts
    shuffles = jax.vmap(lambda single: jax.random.permutation(single, TOK_DEV))(jax.random.split(keys[3], count)).astype(jnp.int32)
    slots = jnp.arange(TOK_DEV, dtype=jnp.int32)
    dest = jnp.sum((ends[:, None, :] <= slots[None, :, None]).astype(jnp.int32), axis=2).astype(jnp.int32)
    within = slots[None, :] - jnp.take_along_axis(starts, dest, axis=1)
    earlier = jnp.cumsum(counts, axis=0) - counts
    packed_pos = dest * TOK_DEV + jnp.take_along_axis(earlier, dest, axis=1) + within
    values = owners[:, None] * TOK_DEV + shuffles
    return jnp.zeros((TOKENS,), jnp.int32).at[packed_pos.reshape(-1)].set(values.reshape(-1))


def draw_doc_start(key, part):
    keys = jax.random.split(jax.random.fold_in(key, 23), 3)
    position = jnp.arange(TOKENS, dtype=jnp.int32)
    long_start = jax.random.randint(keys[0], (), 0, TOKENS - MOST_DOC + 1).astype(jnp.int32)
    period = MOST_DOC // 2
    phase = jax.random.randint(keys[1], (), 0, period).astype(jnp.int32)
    coin = jax.random.randint(keys[2], (TOKENS,), 0, TOK_DEV) == 0
    inside = (position > long_start) & (position < long_start + MOST_DOC)
    cut = ((position % period == phase) | coin) & jnp.logical_not(inside)
    cut = cut | (position == 0) | (position == long_start) | (position == long_start + MOST_DOC)
    return lax.cummax(jnp.where(cut, position, 0).astype(jnp.int32), axis=0)


def draw_memory(key, part):
    single = jax.random.fold_in(key, 37)
    logs = jax.random.uniform(single, (MODES, D), jnp.float32, jnp.log(30.0), jnp.log(32.0 * TOK_DEV))
    return jnp.exp(logs)


def block_scale(key, dims, cuts, low, largest):
    gain = 1.0
    for axis_at, parts in cuts:
        steps = jax.random.uniform(jax.random.fold_in(jax.random.fold_in(key, 6), axis_at), (parts,), jnp.float32, low / len(cuts), largest / len(cuts))
        gain = gain * jnp.repeat(jnp.exp(steps), dims[axis_at] // parts).reshape((-1,) + (1,) * (len(dims) - 1 - axis_at))
    return gain


def gaussian(stream_key, shape, width, limit, cuts=(), kind=jnp.bfloat16):
    values = jax.random.normal(stream_key, shape, jnp.float32) * width
    if len(cuts) > 0:
        values = block_scale(stream_key, shape, cuts, -0.22, 0.18) * values
    return jnp.clip(values, min=-limit, max=limit).astype(kind)


def setup_inputs(seed: int = 0) -> dict:
    streams_of = jax.random.split(jax.random.key(seed), 10)
    fields_in = gaussian(streams_of[0], (TOKENS, 3, D), 1.0, 6.0, ((0, 8), (2, 4)))
    pack_source = draw_pack_source(jax.random.fold_in(streams_of[9], 71), 0)
    doc_start = draw_doc_start(jax.random.fold_in(streams_of[9], 71), 0)
    short_filter = gaussian(streams_of[3], (3, 3, D), 0.6, 2.4, ((2, 4),), jnp.float32)
    memory = draw_memory(jax.random.fold_in(streams_of[9], 71), 0)
    residue = gaussian(streams_of[5], (MODES, D), 1.0, 4.0, ((1, 4),), jnp.float32)
    skip_gain = gaussian(streams_of[6], (D,), 0.5, 2.5, ((0, 4),), jnp.float32)
    w_out = gaussian(streams_of[7], (D, D), D ** -0.5, 0.09375, ((0, 4),))
    cotangent = gaussian(streams_of[8], (TOKENS, D), 1.0, 6.0, ((0, 8), (1, 4)))
    return {"fields_in": fields_in, "pack_source": pack_source, "doc_start": doc_start, "short_filter": short_filter, "memory": memory, "residue": residue, "skip_gain": skip_gain, "w_out": w_out, "cotangent": cotangent}


def reference(fields_in, pack_source, doc_start, short_filter, memory, residue, skip_gain, w_out, cotangent):
    packed = jnp.take(fields_in, pack_source, axis=0)
    position = jnp.arange(TOKENS, dtype=jnp.int32)
    link = (doc_start < position).astype(jnp.float32)
    link_next = jnp.concatenate([link[1:], jnp.zeros((1,), jnp.float32)], axis=0)
    masks = [(position - lag >= doc_start).astype(jnp.float32)[:, None, None] for lag in range(3)]
    decay = jnp.exp(-1.0 / memory)
    norm_gain = jnp.sqrt(1.0 - decay * decay)
    mode_gain = residue * norm_gain
    block = min(512, D)
    count = D // block

    def one_block(mixed_total, index):
        start = index * block
        fields = lax.dynamic_slice_in_dim(packed, start, block, 2).astype(jnp.float32)
        taps = lax.dynamic_slice_in_dim(short_filter, start, block, 2)
        padded = jnp.concatenate([jnp.zeros((2, 3, block), jnp.float32), fields], axis=0)
        lagged = [padded[2 - lag:2 - lag + TOKENS] for lag in range(3)]
        short = masks[0] * taps[None, :, 0, :] * lagged[0]
        for lag in (1, 2):
            short = short + masks[lag] * taps[None, :, lag, :] * lagged[lag]
        query = short[:, 0]
        keys_part = short[:, 1]
        values_part = short[:, 2]
        drive = keys_part * values_part
        decay_block = lax.dynamic_slice_in_dim(decay, start, block, 1)
        gain_block = lax.dynamic_slice_in_dim(mode_gain, start, block, 1)
        norm_block = lax.dynamic_slice_in_dim(norm_gain, start, block, 1)
        skip_block = lax.dynamic_slice_in_dim(skip_gain, start, block, 0)

        def step_forward(carried, inputs):
            value, switch = inputs
            carried = switch * decay_block * carried + value[None]
            return (carried, carried)
        unused, states = lax.scan(step_forward, jnp.zeros((MODES, block), jnp.float32), (drive, link))
        filtered = lax.optimization_barrier(jnp.sum(gain_block[None] * states, axis=1)) + skip_block[None] * drive
        gated = (query * filtered).astype(jnp.bfloat16)
        w_rows = lax.dynamic_slice_in_dim(w_out, start, block, 0)
        mixed_total = mixed_total + jnp.dot(gated, w_rows, preferred_element_type=jnp.float32)
        d_gated = lax.dot_general(cotangent, w_rows, (((1,), (1,)), ((), ())), preferred_element_type=jnp.float32)
        d_query = d_gated * filtered
        d_filtered = d_gated * query

        def step_backward(carried, inputs):
            grad, switch = inputs
            carried = gain_block * grad[None] + switch * decay_block * carried
            return (carried, carried)
        unused_b, adjoints = lax.scan(step_backward, jnp.zeros((MODES, block), jnp.float32), (d_filtered, link_next), reverse=True)
        d_drive = skip_block[None] * d_filtered + lax.optimization_barrier(jnp.sum(adjoints, axis=1))
        d_short = jnp.stack([d_query, d_drive * values_part, d_drive * keys_part], axis=1)
        weighted = [d_short * masks[lag] for lag in range(3)]
        zero_row = jnp.zeros((1, 3, block), jnp.float32)
        d_packed = taps[None, :, 0, :] * weighted[0]
        d_packed = d_packed + taps[None, :, 1, :] * jnp.concatenate([weighted[1][1:], zero_row], axis=0)
        d_packed = d_packed + taps[None, :, 2, :] * jnp.concatenate([weighted[2][2:], zero_row, zero_row], axis=0)
        d_filter_block = jnp.stack([lax.optimization_barrier(jnp.sum(weighted[lag] * lagged[lag], axis=0)) for lag in range(3)], axis=1)
        d_residue_block = norm_block * lax.optimization_barrier(jnp.sum(d_filtered[:, None, :] * states, axis=0))
        d_skip_block = lax.optimization_barrier(jnp.sum(d_filtered * drive, axis=0))
        return (mixed_total, (d_packed.astype(jnp.bfloat16), d_filter_block, d_residue_block, d_skip_block))
    mixed_total, pieces = lax.scan(one_block, jnp.zeros((TOKENS, D), jnp.float32), jnp.arange(count, dtype=jnp.int32))
    d_packed_all = jnp.transpose(pieces[0], (1, 2, 0, 3)).reshape(TOKENS, 3, D)
    d_fields = jnp.zeros((TOKENS, 3, D), jnp.bfloat16).at[pack_source].set(d_packed_all)
    d_filter = jnp.transpose(pieces[1], (1, 2, 0, 3)).reshape(3, 3, D)
    d_residue = jnp.transpose(pieces[2], (1, 0, 2)).reshape(MODES, D)
    d_skip = pieces[3].reshape(D)
    return (mixed_total.astype(jnp.bfloat16), d_fields, d_filter, d_residue, d_skip)
```

```python
import jax
import jax.numpy as jnp
from jax import lax
from jax.experimental import pallas as pl
from jax.experimental.pallas import tpu as pltpu
from jax.sharding import PartitionSpec as P


def shifted(shard, axis, by):
    peers = lax.axis_size(axis)
    pairs = [(i, i + by) for i in range(peers) if 0 <= i + by < peers]
    return lax.ppermute(shard, axis, pairs)


def compose(earlier, later):
    return (earlier[0] * later[0], later[0] * earlier[1] + later[1])


def forward_scan(links, source, axis):
    return lax.associative_scan(compose, (links, source), axis=axis)


def backward_scan(links, source, axis):
    length = links.shape[axis]
    ahead = jnp.concatenate(
        [
            lax.slice_in_dim(links, 1, length, axis=axis),
            jnp.ones_like(lax.slice_in_dim(links, 0, 1, axis=axis)),
        ],
        axis=axis,
    )
    flipped = forward_scan(jnp.flip(ahead, axis), jnp.flip(source, axis), axis)
    return (jnp.flip(flipped[0], axis), jnp.flip(flipped[1], axis))


def rows_of(array, chosen_rows):
    flat = array.reshape(array.shape[0], -1)
    picked = jnp.dot(chosen_rows.astype(array.dtype), flat, preferred_element_type=jnp.float32)
    return picked.astype(array.dtype).reshape((-1,) + array.shape[1:])


def per_device(
    fields_in, pack_source, doc_start, short_filter, memory, residue, skip_gain, w_out, cotangent
):
    rows = fields_in.shape[0]
    width = fields_in.shape[2]
    devices_seq = lax.axis_size("seq")
    here = lax.axis_index("seq")
    capacity = 2 * rows // devices_seq
    source_dev = pack_source // rows
    source_row = pack_source % rows
    line = jnp.arange(rows, dtype=jnp.int32)
    before = (line[:, None] > line[None, :]) & (source_dev[:, None] == source_dev[None, :])
    slot = source_dev * capacity + jnp.sum(before.astype(jnp.int32), axis=1)
    filled = jnp.arange(devices_seq * capacity, dtype=jnp.int32)[:, None] == slot[None, :]
    wanted = jnp.min(jnp.where(filled, source_row[None, :], rows), axis=1)
    wanted = wanted.reshape(devices_seq, capacity)
    asked = lax.all_to_all(wanted, "seq", split_axis=0, concat_axis=0, tiled=True)
    picked = rows_of(fields_in, asked.reshape(-1)[:, None] == line[None, :]).reshape(
        asked.shape[0], asked.shape[1], 3, width
    )
    returned_rows = lax.all_to_all(picked, "seq", split_axis=0, concat_axis=0, tiled=True)
    packed = rows_of(returned_rows.reshape(devices_seq * capacity, 3, width), filled.T)
    position = here * rows + line
    masks = [(position - lag >= doc_start).astype(jnp.float32)[:, None, None] for lag in range(3)]
    tail = shifted(packed[rows - 2 :], "seq", 1)
    extended = jnp.concatenate([tail, packed], axis=0).astype(jnp.float32)
    lagged = [extended[2 - lag : 2 - lag + rows] for lag in range(3)]
    short = masks[0] * short_filter[None, :, 0, :] * lagged[0]
    for lag in (1, 2):
        short = short + masks[lag] * short_filter[None, :, lag, :] * lagged[lag]
    query = short[:, 0]
    keys_part = short[:, 1]
    values_part = short[:, 2]
    drive = keys_part * values_part
    decay = jnp.exp(-1.0 / memory)
    norm_gain = jnp.sqrt(1.0 - decay * decay)
    mode_gain = residue * norm_gain
    part_width = width // devices_seq
    bounds = lax.all_gather(doc_start, "seq", axis=0, tiled=True)
    everywhere = jnp.arange(bounds.shape[0], dtype=jnp.int32)
    link_all = (bounds < everywhere).astype(jnp.float32)
    decay_part = lax.dynamic_slice_in_dim(decay, here * part_width, part_width, 1)
    gain_part = lax.dynamic_slice_in_dim(mode_gain, here * part_width, part_width, 1)
    norm_part = lax.dynamic_slice_in_dim(norm_gain, here * part_width, part_width, 1)
    skip_part = lax.dynamic_slice_in_dim(skip_gain, here * part_width, part_width, 0)
    drive_part = lax.all_to_all(drive.T, "seq", split_axis=0, concat_axis=1, tiled=True)
    links_part = decay_part[:, :, None] * link_all[None, None, :]
    state_part = forward_scan(links_part, jnp.broadcast_to(drive_part[None], links_part.shape), 2)[
        1
    ]
    filtered_part = (
        jnp.sum(gain_part[:, :, None] * state_part, axis=0) + skip_part[:, None] * drive_part
    )
    filtered = lax.all_to_all(filtered_part, "seq", split_axis=1, concat_axis=0, tiled=True).T
    gated = (query * filtered).astype(jnp.bfloat16)
    partial_out = jnp.dot(gated, w_out, preferred_element_type=jnp.float32)
    mixed = lax.psum_scatter(partial_out, "mp", scatter_dimension=1, tiled=True).astype(
        jnp.bfloat16
    )
    d_gated = lax.dot_general(
        lax.all_gather(cotangent, "mp", axis=1, tiled=True),
        w_out,
        (((1,), (1,)), ((), ())),
        preferred_element_type=jnp.float32,
    )
    d_query = d_gated * filtered
    d_filtered = d_gated * query
    grad_part = lax.all_to_all(d_filtered.T, "seq", split_axis=0, concat_axis=1, tiled=True)
    adjoint_part = backward_scan(links_part, gain_part[:, :, None] * grad_part[None], 2)[1]
    back_part = jnp.sum(adjoint_part, axis=0)
    d_drive = (
        skip_gain[None] * d_filtered
        + lax.all_to_all(back_part, "seq", split_axis=1, concat_axis=0, tiled=True).T
    )
    residue_part = norm_part * jnp.sum(grad_part[None] * state_part, axis=2)
    d_residue = lax.all_gather(residue_part, "seq", axis=1, tiled=True)
    d_short = jnp.stack([d_query, d_drive * values_part, d_drive * keys_part], axis=1)
    weighted = [d_short * masks[lag] for lag in range(3)]
    head = jnp.stack(
        [
            short_filter[:, 2, :] * weighted[2][0],
            short_filter[:, 1, :] * weighted[1][0] + short_filter[:, 2, :] * weighted[2][1],
        ],
        axis=0,
    )
    from_next = shifted(head, "seq", -1)
    zero_row = jnp.zeros((1, 3, width), jnp.float32)
    d_packed = short_filter[None, :, 0, :] * weighted[0]
    d_packed = d_packed + short_filter[None, :, 1, :] * jnp.concatenate(
        [weighted[1][1:], zero_row], axis=0
    )
    d_packed = d_packed + short_filter[None, :, 2, :] * jnp.concatenate(
        [weighted[2][2:], zero_row, zero_row], axis=0
    )
    d_packed = d_packed + jnp.concatenate(
        [jnp.zeros((rows - 2, 3, width), jnp.float32), from_next], axis=0
    )
    filter_local = jnp.stack(
        [jnp.sum(weighted[lag] * lagged[lag], axis=0) for lag in range(3)], axis=1
    )
    skip_local = jnp.sum(d_filtered * drive, axis=0)
    d_filter, d_skip = lax.psum((filter_local, skip_local), "seq")
    outgoing = (
        rows_of(d_packed.astype(jnp.bfloat16), filled).reshape(devices_seq, capacity, 3, width)
    )
    returned = lax.all_to_all(outgoing, "seq", split_axis=0, concat_axis=0, tiled=True)
    d_fields = rows_of(returned.reshape(-1, 3, width), line[:, None] == asked.reshape(-1)[None, :])
    return (mixed, d_fields, d_filter, d_residue, d_skip)


PAD = 8
SEGS = 32
LANES = 128


def channel_kernel(
    x_ref, dg_ref, src_col_ref, src_row_ref, rel_ref, taps_ref, memory_ref, residue_ref, skip_ref,
    gated_ref, d_fields_ref, sums_ref,
    x_s, ds_s, dg_s, gated_s, drive_s, k_s, v_s, df_s, dp_s, carry_s,
):
    tokens = x_ref.shape[0]
    steps = tokens // SEGS
    block = 256
    f32 = jnp.float32
    for f in range(3):
        x_s[f, 0:PAD, :] = jnp.zeros((PAD, LANES), f32)
        ds_s[f, PAD + tokens : PAD + tokens + PAD, :] = jnp.zeros((PAD, LANES), f32)
    dg_s[0:tokens, :] = dg_ref[...].astype(f32)

    def gather(i, unused):
        at = pl.multiple_of(i * block, block)
        rows = lax.broadcasted_iota(jnp.int32, (block, tokens), 1)
        pick = jnp.where(src_col_ref[pl.ds(at, block), :] == rows, 1.0, 0.0).astype(jnp.bfloat16)
        got = jnp.dot(pick, x_ref[...], preferred_element_type=f32)
        for f in range(3):
            x_s[f, pl.ds(PAD + at, block), :] = got[:, f * LANES : (f + 1) * LANES]
        return unused

    lax.fori_loop(0, tokens // block, gather, 0)

    decay = [jnp.exp(-1.0 / memory_ref[m : m + 1, :]) for m in range(2)]
    norm = [jnp.sqrt(1.0 - d * d) for d in decay]
    gain = [residue_ref[m : m + 1, :] * norm[m] for m in range(2)]
    whole = [jnp.exp(-float(steps) / memory_ref[m : m + 1, :]) for m in range(2)]
    skip = skip_ref[0:1, :]
    tap = [[taps_ref[3 * f + j : 3 * f + j + 1, :] for j in range(3)] for f in range(3)]

    def at(b, shift=0):
        return pl.ds(PAD + b + shift, SEGS, stride=steps)

    def line(b):
        return pl.ds(pl.multiple_of(b * SEGS, SEGS), SEGS)

    def short(f, b, rel):
        total = tap[f][0] * x_s[f, at(b), :]
        for j in (1, 2):
            total = total + jnp.where(rel >= j, tap[f][j] * x_s[f, at(b, -j), :], 0.0)
        return total

    zero = jnp.zeros((SEGS, LANES), f32)

    def first(b, state):
        rel = rel_ref[at(b), :]
        k = short(1, b, rel)
        v = short(2, b, rel)
        drive = k * v
        k_s[line(b), :] = k
        v_s[line(b), :] = v
        drive_s[line(b), :] = drive
        return tuple(jnp.where(rel >= 1, decay[m] * state[m], 0.0) + drive for m in range(2))

    ends = lax.fori_loop(0, steps, first, (zero, zero), unroll=2)
    joined = rel_ref[at(steps - 1), :] >= steps
    for m in range(2):
        link = jnp.where(joined, whole[m], 0.0)
        carry = jnp.zeros((1, LANES), f32)
        for a in range(SEGS):
            carry_s[m, a : a + 1, :] = carry
            carry = link[a : a + 1, :] * carry + ends[m][a : a + 1, :]

    def second(b, held):
        s0, s1, r0, r1, r2 = held
        rel = rel_ref[at(b), :]
        drive = drive_s[line(b), :]
        s0 = jnp.where(rel >= 1, decay[0] * s0, 0.0) + drive
        s1 = jnp.where(rel >= 1, decay[1] * s1, 0.0) + drive
        filtered = gain[0] * s0 + gain[1] * s1 + skip * drive
        query = short(0, b, rel)
        gated_s[pl.ds(b, SEGS, stride=steps), :] = query * filtered
        dg = dg_s[pl.ds(b, SEGS, stride=steps), :]
        ds_s[0, at(b), :] = dg * filtered
        df = dg * query
        df_s[line(b), :] = df
        return (s0, s1, r0 + df * s0, r1 + df * s1, r2 + df * drive)

    held = (carry_s[0], carry_s[1], zero, zero, zero)
    held = lax.fori_loop(0, steps, second, held, unroll=2)
    gated_ref[...] = gated_s[0:tokens, :].astype(jnp.bfloat16)

    def third(i, adjoint):
        b = steps - 1 - i
        ahead = rel_ref[at(b, 1), :] >= 1
        df = df_s[line(b), :]
        return tuple(gain[m] * df + jnp.where(ahead, decay[m] * adjoint[m], 0.0) for m in range(2))

    starts = lax.fori_loop(0, steps, third, (zero, zero), unroll=2)
    joined = rel_ref[at(0, steps), :] >= steps
    for m in range(2):
        link = jnp.where(joined, whole[m], 0.0)
        carry = jnp.zeros((1, LANES), f32)
        for a in reversed(range(SEGS)):
            carry_s[m, a : a + 1, :] = carry
            carry = link[a : a + 1, :] * carry + starts[m][a : a + 1, :]

    def fourth(i, adjoint):
        b = steps - 1 - i
        ahead = rel_ref[at(b, 1), :] >= 1
        df = df_s[line(b), :]
        adjoint = tuple(
            gain[m] * df + jnp.where(ahead, decay[m] * adjoint[m], 0.0) for m in range(2)
        )
        d_drive = skip * df + adjoint[0] + adjoint[1]
        ds_s[1, at(b), :] = d_drive * v_s[line(b), :]
        ds_s[2, at(b), :] = d_drive * k_s[line(b), :]
        return adjoint

    lax.fori_loop(0, steps, fourth, (carry_s[0], carry_s[1]), unroll=2)

    def fold(value):
        return jnp.sum(value.reshape(SEGS // 8, 8, LANES), axis=0)

    def fifth(b, sums):
        sums = list(sums)
        rel = [rel_ref[at(b, j), :] for j in range(3)]
        for f in range(3):
            here = ds_s[f, at(b), :]
            d_packed = tap[f][0] * here
            sums[3 * f] = sums[3 * f] + fold(here * x_s[f, at(b), :])
            for j in (1, 2):
                d_packed = d_packed + jnp.where(rel[j] >= j, tap[f][j] * ds_s[f, at(b, j), :], 0.0)
                term = jnp.where(rel[0] >= j, here * x_s[f, at(b, -j), :], 0.0)
                sums[3 * f + j] = sums[3 * f + j] + fold(term)
            dp_s[line(b), f * LANES : (f + 1) * LANES] = d_packed.astype(jnp.bfloat16)
        return tuple(sums)

    none = jnp.zeros((8, LANES), f32)
    sums = lax.fori_loop(0, steps, fifth, (none,) * 9)
    for n in range(9):
        sums_ref[n : n + 1, :] = jnp.sum(sums[n], axis=0, keepdims=True)
    for m in range(2):
        sums_ref[9 + m : 10 + m, :] = norm[m] * jnp.sum(held[2 + m], axis=0, keepdims=True)
    sums_ref[11:12, :] = jnp.sum(held[4], axis=0, keepdims=True)
    sums_ref[12:16, :] = jnp.zeros((4, LANES), f32)

    def scatter(i, unused):
        start = pl.multiple_of(i * block, block)
        rows = lax.broadcasted_iota(jnp.int32, (block, tokens), 0) + start
        pick = jnp.where(src_row_ref[...] == rows, 1.0, 0.0).astype(jnp.bfloat16)
        got = jnp.dot(pick, dp_s[...], preferred_element_type=f32)
        d_fields_ref[pl.ds(start, block), :] = got.astype(jnp.bfloat16)
        return unused

    lax.fori_loop(0, tokens // block, scatter, 0)


def channel_part(x, dg, source, starts, taps, memory, residue, skip):
    tokens = x.shape[0]
    steps = tokens // SEGS
    rel = jnp.arange(tokens, dtype=jnp.int32) - starts
    rel = jnp.broadcast_to(jnp.pad(rel, (PAD, PAD + steps))[:, None], (tokens + 2 * PAD + steps, LANES))
    source_row = source.reshape(SEGS, steps).T.reshape(1, tokens)
    f32 = jnp.float32
    padded = tokens + 2 * PAD + steps
    return pl.pallas_call(
        channel_kernel,
        out_shape=(
            jax.ShapeDtypeStruct((tokens, LANES), jnp.bfloat16),
            jax.ShapeDtypeStruct((tokens, 3 * LANES), jnp.bfloat16),
            jax.ShapeDtypeStruct((16, LANES), f32),
        ),
        scratch_shapes=[
            pltpu.VMEM((3, padded, LANES), f32),
            pltpu.VMEM((3, padded, LANES), f32),
            pltpu.VMEM((tokens + steps, LANES), f32),
            pltpu.VMEM((tokens + steps, LANES), f32),
            pltpu.VMEM((tokens, LANES), f32),
            pltpu.VMEM((tokens, LANES), f32),
            pltpu.VMEM((tokens, LANES), f32),
            pltpu.VMEM((tokens, LANES), f32),
            pltpu.VMEM((tokens, 3 * LANES), jnp.bfloat16),
            pltpu.VMEM((2, SEGS, LANES), f32),
        ],
        compiler_params=pltpu.CompilerParams(vmem_limit_bytes=48 * 1024 * 1024),
        name="channel_part",
    )(x, dg, source[:, None], source_row, rel, taps, memory, residue, skip)


def by_channels(
    fields_in, pack_source, doc_start, short_filter, memory, residue, skip_gain, w_out, cotangent
):
    rows, _, width = fields_in.shape
    peers = lax.axis_size("seq")
    here = lax.axis_index("seq")
    tokens = rows * peers
    part = width // peers

    def exchange(shard):
        return lax.all_to_all(shard, "seq", split_axis=0, concat_axis=0, tiled=True)

    x = exchange(
        fields_in.reshape(rows, 3, peers, part).transpose(2, 0, 1, 3).reshape(peers, rows, 3 * part)
    ).reshape(tokens, 3 * part)
    ints = lax.all_gather(jnp.stack([pack_source, doc_start]), "seq", axis=1, tiled=True)
    d_gated = lax.dot_general(
        lax.all_gather(cotangent, "mp", axis=1, tiled=True),
        w_out,
        (((1,), (1,)), ((), ())),
        preferred_element_type=jnp.float32,
    ).astype(jnp.bfloat16)
    dg = exchange(d_gated.reshape(rows, peers, part).transpose(1, 0, 2)).reshape(tokens, part)

    def own(array):
        return lax.dynamic_slice_in_dim(array, here * part, part, array.ndim - 1)

    gated, d_fields, sums = channel_part(
        x,
        dg,
        ints[0],
        ints[1],
        own(short_filter).reshape(9, part),
        own(memory),
        own(residue),
        own(skip_gain).reshape(1, part),
    )
    gated = exchange(gated.reshape(peers, rows, part)).transpose(1, 0, 2).reshape(rows, width)
    d_fields = exchange(d_fields.reshape(peers, rows, 3 * part))
    d_fields = d_fields.reshape(peers, rows, 3, part).transpose(1, 2, 0, 3).reshape(rows, 3, width)
    partial_out = jnp.dot(gated, w_out, preferred_element_type=jnp.float32)
    mixed = lax.psum_scatter(partial_out, "mp", scatter_dimension=1, tiled=True).astype(
        jnp.bfloat16
    )
    sums = lax.all_gather(sums, "seq", axis=1, tiled=True)
    return (mixed, d_fields, sums[:9].reshape(3, 3, width), sums[9:11], sums[11])


def chosen(*arrays):
    rows, _, width = arrays[0].shape
    peers = lax.axis_size("seq")
    if width == LANES * peers and rows * peers <= 4096 and rows % 256 == 0:
        return by_channels(*arrays)
    return per_device(*arrays)


def solution(mesh):
    placed = (
        P("seq", None, "mp"),
        P("seq"),
        P("seq"),
        P(None, None, "mp"),
        P(None, "mp"),
        P(None, "mp"),
        P("mp"),
        P("mp", None),
        P("seq", "mp"),
    )
    return jax.shard_map(
        chosen,
        mesh=mesh,
        in_specs=placed,
        out_specs=(
            P("seq", "mp"),
            P("seq", None, "mp"),
            P(None, None, "mp"),
            P(None, "mp"),
            P("mp"),
        ),
        check_vma=False,
    )
```

```python
import jax
import jax.numpy as jnp
from jax import lax
from jax.experimental import pallas as pl
from jax.experimental.pallas import tpu as pltpu
from jax.sharding import PartitionSpec as P


def shifted(shard, axis, by):
    peers = lax.axis_size(axis)
    pairs = [(i, i + by) for i in range(peers) if 0 <= i + by < peers]
    return lax.ppermute(shard, axis, pairs)


def compose(earlier, later):
    return (earlier[0] * later[0], later[0] * earlier[1] + later[1])


def forward_scan(links, source, axis):
    return lax.associative_scan(compose, (links, source), axis=axis)


def backward_scan(links, source, axis):
    length = links.shape[axis]
    ahead = jnp.concatenate(
        [
            lax.slice_in_dim(links, 1, length, axis=axis),
            jnp.ones_like(lax.slice_in_dim(links, 0, 1, axis=axis)),
        ],
        axis=axis,
    )
    flipped = forward_scan(jnp.flip(ahead, axis), jnp.flip(source, axis), axis)
    return (jnp.flip(flipped[0], axis), jnp.flip(flipped[1], axis))


def rows_of(array, chosen_rows):
    flat = array.reshape(array.shape[0], -1)
    picked = jnp.dot(chosen_rows.astype(array.dtype), flat, preferred_element_type=jnp.float32)
    return picked.astype(array.dtype).reshape((-1,) + array.shape[1:])


def per_device(
    fields_in, pack_source, doc_start, short_filter, memory, residue, skip_gain, w_out, cotangent
):
    rows = fields_in.shape[0]
    width = fields_in.shape[2]
    devices_seq = lax.axis_size("seq")
    here = lax.axis_index("seq")
    capacity = 2 * rows // devices_seq
    source_dev = pack_source // rows
    source_row = pack_source % rows
    line = jnp.arange(rows, dtype=jnp.int32)
    before = (line[:, None] > line[None, :]) & (source_dev[:, None] == source_dev[None, :])
    slot = source_dev * capacity + jnp.sum(before.astype(jnp.int32), axis=1)
    filled = jnp.arange(devices_seq * capacity, dtype=jnp.int32)[:, None] == slot[None, :]
    wanted = jnp.min(jnp.where(filled, source_row[None, :], rows), axis=1)
    wanted = wanted.reshape(devices_seq, capacity)
    asked = lax.all_to_all(wanted, "seq", split_axis=0, concat_axis=0, tiled=True)
    picked = rows_of(fields_in, asked.reshape(-1)[:, None] == line[None, :]).reshape(
        asked.shape[0], asked.shape[1], 3, width
    )
    returned_rows = lax.all_to_all(picked, "seq", split_axis=0, concat_axis=0, tiled=True)
    packed = rows_of(returned_rows.reshape(devices_seq * capacity, 3, width), filled.T)
    position = here * rows + line
    masks = [(position - lag >= doc_start).astype(jnp.float32)[:, None, None] for lag in range(3)]
    tail = shifted(packed[rows - 2 :], "seq", 1)
    extended = jnp.concatenate([tail, packed], axis=0).astype(jnp.float32)
    lagged = [extended[2 - lag : 2 - lag + rows] for lag in range(3)]
    short = masks[0] * short_filter[None, :, 0, :] * lagged[0]
    for lag in (1, 2):
        short = short + masks[lag] * short_filter[None, :, lag, :] * lagged[lag]
    query = short[:, 0]
    keys_part = short[:, 1]
    values_part = short[:, 2]
    drive = keys_part * values_part
    decay = jnp.exp(-1.0 / memory)
    norm_gain = jnp.sqrt(1.0 - decay * decay)
    mode_gain = residue * norm_gain
    part_width = width // devices_seq
    bounds = lax.all_gather(doc_start, "seq", axis=0, tiled=True)
    everywhere = jnp.arange(bounds.shape[0], dtype=jnp.int32)
    link_all = (bounds < everywhere).astype(jnp.float32)
    decay_part = lax.dynamic_slice_in_dim(decay, here * part_width, part_width, 1)
    gain_part = lax.dynamic_slice_in_dim(mode_gain, here * part_width, part_width, 1)
    norm_part = lax.dynamic_slice_in_dim(norm_gain, here * part_width, part_width, 1)
    skip_part = lax.dynamic_slice_in_dim(skip_gain, here * part_width, part_width, 0)
    drive_part = lax.all_to_all(drive.T, "seq", split_axis=0, concat_axis=1, tiled=True)
    links_part = decay_part[:, :, None] * link_all[None, None, :]
    state_part = forward_scan(links_part, jnp.broadcast_to(drive_part[None], links_part.shape), 2)[
        1
    ]
    filtered_part = (
        jnp.sum(gain_part[:, :, None] * state_part, axis=0) + skip_part[:, None] * drive_part
    )
    filtered = lax.all_to_all(filtered_part, "seq", split_axis=1, concat_axis=0, tiled=True).T
    gated = (query * filtered).astype(jnp.bfloat16)
    partial_out = jnp.dot(gated, w_out, preferred_element_type=jnp.float32)
    mixed = lax.psum_scatter(partial_out, "mp", scatter_dimension=1, tiled=True).astype(
        jnp.bfloat16
    )
    d_gated = lax.dot_general(
        lax.all_gather(cotangent, "mp", axis=1, tiled=True),
        w_out,
        (((1,), (1,)), ((), ())),
        preferred_element_type=jnp.float32,
    )
    d_query = d_gated * filtered
    d_filtered = d_gated * query
    grad_part = lax.all_to_all(d_filtered.T, "seq", split_axis=0, concat_axis=1, tiled=True)
    adjoint_part = backward_scan(links_part, gain_part[:, :, None] * grad_part[None], 2)[1]
    back_part = jnp.sum(adjoint_part, axis=0)
    d_drive = (
        skip_gain[None] * d_filtered
        + lax.all_to_all(back_part, "seq", split_axis=1, concat_axis=0, tiled=True).T
    )
    residue_part = norm_part * jnp.sum(grad_part[None] * state_part, axis=2)
    d_residue = lax.all_gather(residue_part, "seq", axis=1, tiled=True)
    d_short = jnp.stack([d_query, d_drive * values_part, d_drive * keys_part], axis=1)
    weighted = [d_short * masks[lag] for lag in range(3)]
    head = jnp.stack(
        [
            short_filter[:, 2, :] * weighted[2][0],
            short_filter[:, 1, :] * weighted[1][0] + short_filter[:, 2, :] * weighted[2][1],
        ],
        axis=0,
    )
    from_next = shifted(head, "seq", -1)
    zero_row = jnp.zeros((1, 3, width), jnp.float32)
    d_packed = short_filter[None, :, 0, :] * weighted[0]
    d_packed = d_packed + short_filter[None, :, 1, :] * jnp.concatenate(
        [weighted[1][1:], zero_row], axis=0
    )
    d_packed = d_packed + short_filter[None, :, 2, :] * jnp.concatenate(
        [weighted[2][2:], zero_row, zero_row], axis=0
    )
    d_packed = d_packed + jnp.concatenate(
        [jnp.zeros((rows - 2, 3, width), jnp.float32), from_next], axis=0
    )
    filter_local = jnp.stack(
        [jnp.sum(weighted[lag] * lagged[lag], axis=0) for lag in range(3)], axis=1
    )
    skip_local = jnp.sum(d_filtered * drive, axis=0)
    d_filter, d_skip = lax.psum((filter_local, skip_local), "seq")
    outgoing = (
        rows_of(d_packed.astype(jnp.bfloat16), filled).reshape(devices_seq, capacity, 3, width)
    )
    returned = lax.all_to_all(outgoing, "seq", split_axis=0, concat_axis=0, tiled=True)
    d_fields = rows_of(returned.reshape(-1, 3, width), line[:, None] == asked.reshape(-1)[None, :])
    return (mixed, d_fields, d_filter, d_residue, d_skip)


EXTRA = 16
PAD = 8
SEGS = 32
LANES = 128


def channel_kernel(
    x_ref, dg_ref, src_col_ref, src_row_ref, rel_ref, taps_ref, memory_ref, residue_ref, skip_ref,
    gated_ref, d_fields_ref,
    x_s, ds_s, dg_s, gated_s, drive_s, k_s, v_s, df_s, dp_s, carry_s, sums_s,
):
    tokens = gated_ref.shape[0]
    peers = d_fields_ref.shape[0]
    share = tokens // peers
    steps = tokens // SEGS
    block = 256
    f32 = jnp.float32
    for f in range(3):
        x_s[f, 0:PAD, :] = jnp.zeros((PAD, LANES), f32)
        ds_s[f, PAD + tokens : PAD + tokens + PAD, :] = jnp.zeros((PAD, LANES), f32)
    dg_s[0:tokens, :] = dg_ref[...].astype(f32)

    def gather(i, unused):
        at = pl.multiple_of(i * block, block)
        rows = lax.broadcasted_iota(jnp.int32, (block, x_ref.shape[0]), 1)
        pick = jnp.where(src_col_ref[pl.ds(at, block), :] == rows, 1.0, 0.0).astype(jnp.bfloat16)
        got = jnp.dot(pick, x_ref[...], preferred_element_type=f32)
        for f in range(3):
            x_s[f, pl.ds(PAD + at, block), :] = got[:, f * LANES : (f + 1) * LANES]
        return unused

    lax.fori_loop(0, tokens // block, gather, 0)

    decay = [jnp.exp(-1.0 / memory_ref[m : m + 1, :]) for m in range(2)]
    norm = [jnp.sqrt(1.0 - d * d) for d in decay]
    gain = [residue_ref[m : m + 1, :] * norm[m] for m in range(2)]
    whole = [jnp.exp(-float(steps) / memory_ref[m : m + 1, :]) for m in range(2)]
    skip = skip_ref[0:1, :]
    tap = [[taps_ref[3 * f + j : 3 * f + j + 1, :] for j in range(3)] for f in range(3)]

    def at(b, shift=0):
        return pl.ds(PAD + b + shift, SEGS, stride=steps)

    def line(b):
        return pl.ds(pl.multiple_of(b * SEGS, SEGS), SEGS)

    def short(f, b, rel):
        total = tap[f][0] * x_s[f, at(b), :]
        for j in (1, 2):
            total = total + jnp.where(rel >= j, tap[f][j] * x_s[f, at(b, -j), :], 0.0)
        return total

    zero = jnp.zeros((SEGS, LANES), f32)

    def first(b, state):
        rel = rel_ref[at(b), :]
        k = short(1, b, rel)
        v = short(2, b, rel)
        drive = k * v
        k_s[line(b), :] = k
        v_s[line(b), :] = v
        drive_s[line(b), :] = drive
        return tuple(jnp.where(rel >= 1, decay[m] * state[m], 0.0) + drive for m in range(2))

    ends = lax.fori_loop(0, steps, first, (zero, zero), unroll=2)
    joined = rel_ref[at(steps - 1), :] >= steps
    for m in range(2):
        link = jnp.where(joined, whole[m], 0.0)
        carry = jnp.zeros((1, LANES), f32)
        for a in range(SEGS):
            carry_s[m, a : a + 1, :] = carry
            carry = link[a : a + 1, :] * carry + ends[m][a : a + 1, :]

    def second(b, held):
        s0, s1, r0, r1, r2 = held
        rel = rel_ref[at(b), :]
        drive = drive_s[line(b), :]
        s0 = jnp.where(rel >= 1, decay[0] * s0, 0.0) + drive
        s1 = jnp.where(rel >= 1, decay[1] * s1, 0.0) + drive
        filtered = gain[0] * s0 + gain[1] * s1 + skip * drive
        query = short(0, b, rel)
        gated_s[pl.ds(b, SEGS, stride=steps), :] = query * filtered
        dg = dg_s[pl.ds(b, SEGS, stride=steps), :]
        ds_s[0, at(b), :] = dg * filtered
        df = dg * query
        df_s[line(b), :] = df
        return (s0, s1, r0 + df * s0, r1 + df * s1, r2 + df * drive)

    held = (carry_s[0], carry_s[1], zero, zero, zero)
    held = lax.fori_loop(0, steps, second, held, unroll=2)
    gated_ref[...] = gated_s[0:tokens, :].astype(jnp.bfloat16)

    def third(i, adjoint):
        b = steps - 1 - i
        ahead = rel_ref[at(b, 1), :] >= 1
        df = df_s[line(b), :]
        return tuple(gain[m] * df + jnp.where(ahead, decay[m] * adjoint[m], 0.0) for m in range(2))

    starts = lax.fori_loop(0, steps, third, (zero, zero), unroll=2)
    joined = rel_ref[at(0, steps), :] >= steps
    for m in range(2):
        link = jnp.where(joined, whole[m], 0.0)
        carry = jnp.zeros((1, LANES), f32)
        for a in reversed(range(SEGS)):
            carry_s[m, a : a + 1, :] = carry
            carry = link[a : a + 1, :] * carry + starts[m][a : a + 1, :]

    def fourth(i, adjoint):
        b = steps - 1 - i
        ahead = rel_ref[at(b, 1), :] >= 1
        df = df_s[line(b), :]
        adjoint = tuple(
            gain[m] * df + jnp.where(ahead, decay[m] * adjoint[m], 0.0) for m in range(2)
        )
        d_drive = skip * df + adjoint[0] + adjoint[1]
        ds_s[1, at(b), :] = d_drive * v_s[line(b), :]
        ds_s[2, at(b), :] = d_drive * k_s[line(b), :]
        return adjoint

    lax.fori_loop(0, steps, fourth, (carry_s[0], carry_s[1]), unroll=2)

    def fold(value):
        return jnp.sum(value.reshape(SEGS // 8, 8, LANES), axis=0)

    def fifth(b, sums):
        sums = list(sums)
        rel = [rel_ref[at(b, j), :] for j in range(3)]
        for f in range(3):
            here = ds_s[f, at(b), :]
            d_packed = tap[f][0] * here
            sums[3 * f] = sums[3 * f] + fold(here * x_s[f, at(b), :])
            for j in (1, 2):
                d_packed = d_packed + jnp.where(rel[j] >= j, tap[f][j] * ds_s[f, at(b, j), :], 0.0)
                term = jnp.where(rel[0] >= j, here * x_s[f, at(b, -j), :], 0.0)
                sums[3 * f + j] = sums[3 * f + j] + fold(term)
            dp_s[line(b), f * LANES : (f + 1) * LANES] = d_packed.astype(jnp.bfloat16)
        return tuple(sums)

    none = jnp.zeros((8, LANES), f32)
    sums = lax.fori_loop(0, steps, fifth, (none,) * 9)
    for n in range(9):
        sums_s[n : n + 1, :] = jnp.sum(sums[n], axis=0, keepdims=True)
    for m in range(2):
        sums_s[9 + m : 10 + m, :] = norm[m] * jnp.sum(held[2 + m], axis=0, keepdims=True)
    sums_s[11:12, :] = jnp.sum(held[4], axis=0, keepdims=True)
    sums_s[12:16, :] = jnp.zeros((4, LANES), f32)
    rest = sums_s[...]
    for f in range(3):
        part = rest.astype(jnp.bfloat16)
        rest = rest - part.astype(f32)
        for d in range(peers):
            d_fields_ref[d, share : share + EXTRA, f * LANES : (f + 1) * LANES] = part

    def scatter(i, unused):
        start = pl.multiple_of(i * block, block)
        rows = lax.broadcasted_iota(jnp.int32, (block, tokens), 0) + start
        pick = jnp.where(src_row_ref[...] == rows, 1.0, 0.0).astype(jnp.bfloat16)
        got = jnp.dot(pick, dp_s[...], preferred_element_type=f32)
        d_fields_ref[i // (share // block), pl.ds(start % share, block), :] = got.astype(jnp.bfloat16)
        return unused

    lax.fori_loop(0, tokens // block, scatter, 0)


def channel_part(x, dg, source, starts, taps, memory, residue, skip, peers):
    tokens = dg.shape[0]
    share = tokens // peers
    steps = tokens // SEGS
    rel = jnp.arange(tokens, dtype=jnp.int32) - starts
    rel = jnp.broadcast_to(jnp.pad(rel, (PAD, PAD + steps))[:, None], (tokens + 2 * PAD + steps, LANES))
    source_row = source.reshape(SEGS, steps).T.reshape(1, tokens)
    f32 = jnp.float32
    padded = tokens + 2 * PAD + steps
    return pl.pallas_call(
        channel_kernel,
        out_shape=(
            jax.ShapeDtypeStruct((tokens, LANES), jnp.bfloat16),
            jax.ShapeDtypeStruct((peers, share + EXTRA, 3 * LANES), jnp.bfloat16),
        ),
        scratch_shapes=[
            pltpu.VMEM((3, padded, LANES), f32),
            pltpu.VMEM((3, padded, LANES), f32),
            pltpu.VMEM((tokens + steps, LANES), f32),
            pltpu.VMEM((tokens + steps, LANES), f32),
            pltpu.VMEM((tokens, LANES), f32),
            pltpu.VMEM((tokens, LANES), f32),
            pltpu.VMEM((tokens, LANES), f32),
            pltpu.VMEM((tokens, LANES), f32),
            pltpu.VMEM((tokens, 3 * LANES), jnp.bfloat16),
            pltpu.VMEM((2, SEGS, LANES), f32),
            pltpu.VMEM((EXTRA, LANES), f32),
        ],
        compiler_params=pltpu.CompilerParams(vmem_limit_bytes=48 * 1024 * 1024),
        name="channel_part",
    )(x, dg, (source + EXTRA * (source // share))[:, None], source_row, rel, taps, memory, residue, skip)


def by_channels(
    fields_in, pack_source, doc_start, short_filter, memory, residue, skip_gain, w_out, cotangent
):
    rows, _, width = fields_in.shape
    peers = lax.axis_size("seq")
    here = lax.axis_index("seq")
    tokens = rows * peers
    part = width // peers

    def exchange(shard):
        return lax.all_to_all(shard, "seq", split_axis=0, concat_axis=0, tiled=True)

    fields = fields_in.reshape(rows, 3, peers, part).transpose(2, 0, 1, 3)
    ints = jnp.concatenate([pack_source, doc_start])
    digits = jnp.concatenate([ints // 128, ints % 128]).astype(jnp.bfloat16)
    digits = jnp.pad(digits, (0, EXTRA * 3 * part - digits.shape[0])).reshape(1, EXTRA, 3 * part)
    digits = jnp.broadcast_to(digits, (peers, EXTRA, 3 * part))
    x = exchange(jnp.concatenate([fields.reshape(peers, rows, 3 * part), digits], axis=1))
    digits = x[:, rows:].reshape(peers, EXTRA * 3 * part)[:, : 4 * rows].astype(jnp.int32)
    ints = digits[:, : 2 * rows] * 128 + digits[:, 2 * rows :]
    x = x.reshape(-1, 3 * part)
    d_gated = lax.dot_general(
        lax.all_gather(cotangent, "mp", axis=1, tiled=True),
        w_out,
        (((1,), (1,)), ((), ())),
        preferred_element_type=jnp.float32,
    ).astype(jnp.bfloat16)
    dg = exchange(d_gated.reshape(rows, peers, part).transpose(1, 0, 2)).reshape(tokens, part)

    def own(array):
        return lax.dynamic_slice_in_dim(array, here * part, part, array.ndim - 1)

    gated, d_fields = channel_part(
        x,
        dg,
        ints[:, :rows].reshape(tokens),
        ints[:, rows:].reshape(tokens),
        own(short_filter).reshape(9, part),
        own(memory),
        own(residue),
        own(skip_gain).reshape(1, part),
        peers,
    )
    gated = exchange(gated.reshape(peers, rows, part)).transpose(1, 0, 2).reshape(rows, width)
    arrived = exchange(d_fields)
    d_fields = arrived[:, :rows].reshape(peers, rows, 3, part).transpose(1, 2, 0, 3).reshape(rows, 3, width)
    partial_out = jnp.dot(gated, w_out, preferred_element_type=jnp.float32)
    mixed = lax.psum_scatter(partial_out, "mp", scatter_dimension=1, tiled=True).astype(
        jnp.bfloat16
    )
    sums = arrived[:, rows:].reshape(peers, EXTRA, 3, part).astype(jnp.float32).sum(axis=2)
    sums = sums.transpose(1, 0, 2).reshape(EXTRA, width)
    return (mixed, d_fields, sums[:9].reshape(3, 3, width), sums[9:11], sums[11])


def chosen(*arrays):
    rows, _, width = arrays[0].shape
    peers = lax.axis_size("seq")
    if width == LANES * peers and rows * peers <= 4096 and rows % 256 == 0 and 4 * rows <= EXTRA * 3 * LANES:
        return by_channels(*arrays)
    return per_device(*arrays)


def solution(mesh):
    placed = (
        P("seq", None, "mp"),
        P("seq"),
        P("seq"),
        P(None, None, "mp"),
        P(None, "mp"),
        P(None, "mp"),
        P("mp"),
        P("mp", None),
        P("seq", "mp"),
    )
    return jax.shard_map(
        chosen,
        mesh=mesh,
        in_specs=placed,
        out_specs=(
            P("seq", "mp"),
            P("seq", None, "mp"),
            P(None, None, "mp"),
            P(None, "mp"),
            P("mp"),
        ),
        check_vma=False,
    )
```

```python
import jax
import jax.numpy as jnp
from jax import lax
from jax.experimental import pallas as pl
from jax.experimental.pallas import tpu as pltpu
from jax.sharding import PartitionSpec as P


def shifted(shard, axis, by):
    peers = lax.axis_size(axis)
    pairs = [(i, i + by) for i in range(peers) if 0 <= i + by < peers]
    return lax.ppermute(shard, axis, pairs)


def compose(earlier, later):
    return (earlier[0] * later[0], later[0] * earlier[1] + later[1])


def forward_scan(links, source, axis):
    return lax.associative_scan(compose, (links, source), axis=axis)


def backward_scan(links, source, axis):
    length = links.shape[axis]
    ahead = jnp.concatenate(
        [
            lax.slice_in_dim(links, 1, length, axis=axis),
            jnp.ones_like(lax.slice_in_dim(links, 0, 1, axis=axis)),
        ],
        axis=axis,
    )
    flipped = forward_scan(jnp.flip(ahead, axis), jnp.flip(source, axis), axis)
    return (jnp.flip(flipped[0], axis), jnp.flip(flipped[1], axis))


def rows_of(array, chosen_rows):
    flat = array.reshape(array.shape[0], -1)
    picked = jnp.dot(chosen_rows.astype(array.dtype), flat, preferred_element_type=jnp.float32)
    return picked.astype(array.dtype).reshape((-1,) + array.shape[1:])


def per_device(
    fields_in, pack_source, doc_start, short_filter, memory, residue, skip_gain, w_out, cotangent
):
    rows = fields_in.shape[0]
    width = fields_in.shape[2]
    devices_seq = lax.axis_size("seq")
    here = lax.axis_index("seq")
    capacity = 2 * rows // devices_seq
    source_dev = pack_source // rows
    source_row = pack_source % rows
    line = jnp.arange(rows, dtype=jnp.int32)
    before = (line[:, None] > line[None, :]) & (source_dev[:, None] == source_dev[None, :])
    slot = source_dev * capacity + jnp.sum(before.astype(jnp.int32), axis=1)
    filled = jnp.arange(devices_seq * capacity, dtype=jnp.int32)[:, None] == slot[None, :]
    wanted = jnp.min(jnp.where(filled, source_row[None, :], rows), axis=1)
    wanted = wanted.reshape(devices_seq, capacity)
    asked = lax.all_to_all(wanted, "seq", split_axis=0, concat_axis=0, tiled=True)
    picked = rows_of(fields_in, asked.reshape(-1)[:, None] == line[None, :]).reshape(
        asked.shape[0], asked.shape[1], 3, width
    )
    returned_rows = lax.all_to_all(picked, "seq", split_axis=0, concat_axis=0, tiled=True)
    packed = rows_of(returned_rows.reshape(devices_seq * capacity, 3, width), filled.T)
    position = here * rows + line
    masks = [(position - lag >= doc_start).astype(jnp.float32)[:, None, None] for lag in range(3)]
    tail = shifted(packed[rows - 2 :], "seq", 1)
    extended = jnp.concatenate([tail, packed], axis=0).astype(jnp.float32)
    lagged = [extended[2 - lag : 2 - lag + rows] for lag in range(3)]
    short = masks[0] * short_filter[None, :, 0, :] * lagged[0]
    for lag in (1, 2):
        short = short + masks[lag] * short_filter[None, :, lag, :] * lagged[lag]
    query = short[:, 0]
    keys_part = short[:, 1]
    values_part = short[:, 2]
    drive = keys_part * values_part
    decay = jnp.exp(-1.0 / memory)
    norm_gain = jnp.sqrt(1.0 - decay * decay)
    mode_gain = residue * norm_gain
    part_width = width // devices_seq
    bounds = lax.all_gather(doc_start, "seq", axis=0, tiled=True)
    everywhere = jnp.arange(bounds.shape[0], dtype=jnp.int32)
    link_all = (bounds < everywhere).astype(jnp.float32)
    decay_part = lax.dynamic_slice_in_dim(decay, here * part_width, part_width, 1)
    gain_part = lax.dynamic_slice_in_dim(mode_gain, here * part_width, part_width, 1)
    norm_part = lax.dynamic_slice_in_dim(norm_gain, here * part_width, part_width, 1)
    skip_part = lax.dynamic_slice_in_dim(skip_gain, here * part_width, part_width, 0)
    drive_part = lax.all_to_all(drive.T, "seq", split_axis=0, concat_axis=1, tiled=True)
    links_part = decay_part[:, :, None] * link_all[None, None, :]
    state_part = forward_scan(links_part, jnp.broadcast_to(drive_part[None], links_part.shape), 2)[
        1
    ]
    filtered_part = (
        jnp.sum(gain_part[:, :, None] * state_part, axis=0) + skip_part[:, None] * drive_part
    )
    filtered = lax.all_to_all(filtered_part, "seq", split_axis=1, concat_axis=0, tiled=True).T
    gated = (query * filtered).astype(jnp.bfloat16)
    partial_out = jnp.dot(gated, w_out, preferred_element_type=jnp.float32)
    mixed = lax.psum_scatter(partial_out, "mp", scatter_dimension=1, tiled=True).astype(
        jnp.bfloat16
    )
    d_gated = lax.dot_general(
        lax.all_gather(cotangent, "mp", axis=1, tiled=True),
        w_out,
        (((1,), (1,)), ((), ())),
        preferred_element_type=jnp.float32,
    )
    d_query = d_gated * filtered
    d_filtered = d_gated * query
    grad_part = lax.all_to_all(d_filtered.T, "seq", split_axis=0, concat_axis=1, tiled=True)
    adjoint_part = backward_scan(links_part, gain_part[:, :, None] * grad_part[None], 2)[1]
    back_part = jnp.sum(adjoint_part, axis=0)
    d_drive = (
        skip_gain[None] * d_filtered
        + lax.all_to_all(back_part, "seq", split_axis=1, concat_axis=0, tiled=True).T
    )
    residue_part = norm_part * jnp.sum(grad_part[None] * state_part, axis=2)
    d_residue = lax.all_gather(residue_part, "seq", axis=1, tiled=True)
    d_short = jnp.stack([d_query, d_drive * values_part, d_drive * keys_part], axis=1)
    weighted = [d_short * masks[lag] for lag in range(3)]
    head = jnp.stack(
        [
            short_filter[:, 2, :] * weighted[2][0],
            short_filter[:, 1, :] * weighted[1][0] + short_filter[:, 2, :] * weighted[2][1],
        ],
        axis=0,
    )
    from_next = shifted(head, "seq", -1)
    zero_row = jnp.zeros((1, 3, width), jnp.float32)
    d_packed = short_filter[None, :, 0, :] * weighted[0]
    d_packed = d_packed + short_filter[None, :, 1, :] * jnp.concatenate(
        [weighted[1][1:], zero_row], axis=0
    )
    d_packed = d_packed + short_filter[None, :, 2, :] * jnp.concatenate(
        [weighted[2][2:], zero_row, zero_row], axis=0
    )
    d_packed = d_packed + jnp.concatenate(
        [jnp.zeros((rows - 2, 3, width), jnp.float32), from_next], axis=0
    )
    filter_local = jnp.stack(
        [jnp.sum(weighted[lag] * lagged[lag], axis=0) for lag in range(3)], axis=1
    )
    skip_local = jnp.sum(d_filtered * drive, axis=0)
    d_filter, d_skip = lax.psum((filter_local, skip_local), "seq")
    outgoing = (
        rows_of(d_packed.astype(jnp.bfloat16), filled).reshape(devices_seq, capacity, 3, width)
    )
    returned = lax.all_to_all(outgoing, "seq", split_axis=0, concat_axis=0, tiled=True)
    d_fields = rows_of(returned.reshape(-1, 3, width), line[:, None] == asked.reshape(-1)[None, :])
    return (mixed, d_fields, d_filter, d_residue, d_skip)


EXTRA = 16
PAD = 8
SEGS = 32
LANES = 128


def at(b, steps, shift=0):
    return pl.ds(PAD + b + shift, SEGS, stride=steps)


def line(b):
    return pl.ds(pl.multiple_of(b * SEGS, SEGS), SEGS)


def modes_of(memory_ref, residue_ref, steps):
    decay = [jnp.exp(-1.0 / memory_ref[m : m + 1, :]) for m in range(2)]
    norm = [jnp.sqrt(1.0 - d * d) for d in decay]
    gain = [residue_ref[m : m + 1, :] * norm[m] for m in range(2)]
    whole = [jnp.exp(-float(steps) / memory_ref[m : m + 1, :]) for m in range(2)]
    return decay, norm, gain, whole


def taps_of(taps_ref):
    return [[taps_ref[3 * f + j : 3 * f + j + 1, :] for j in range(3)] for f in range(3)]


def short_of(x_s, tap, steps, f, b, rel):
    total = tap[f][0] * x_s[f, at(b, steps), :]
    for j in (1, 2):
        total = total + jnp.where(rel >= j, tap[f][j] * x_s[f, at(b, steps, -j), :], 0.0)
    return total


def forward_kernel(
    x_ref, src_col_ref, rel_ref, taps_ref, memory_ref, residue_ref, skip_ref,
    gated_ref, x_s, k_s, v_s, drive_s, filtered_s, state_s,
    gated_s, carry_s,
):
    tokens = gated_ref.shape[0]
    steps = tokens // SEGS
    block = 256
    f32 = jnp.float32
    for f in range(3):
        x_s[f, 0:PAD, :] = jnp.zeros((PAD, LANES), f32)
        x_s[f, PAD + tokens :, :] = jnp.zeros((x_s.shape[1] - PAD - tokens, LANES), f32)

    def gather(i, unused):
        at = pl.multiple_of(i * block, block)
        rows = lax.broadcasted_iota(jnp.int32, (block, x_ref.shape[0]), 1)
        pick = jnp.where(src_col_ref[pl.ds(at, block), :] == rows, 1.0, 0.0).astype(jnp.bfloat16)
        got = jnp.dot(pick, x_ref[...], preferred_element_type=f32)
        for f in range(3):
            x_s[f, pl.ds(PAD + at, block), :] = got[:, f * LANES : (f + 1) * LANES]
        return unused

    lax.fori_loop(0, tokens // block, gather, 0)

    decay, norm, gain, whole = modes_of(memory_ref, residue_ref, steps)
    skip = skip_ref[0:1, :]
    tap = taps_of(taps_ref)

    zero = jnp.zeros((SEGS, LANES), f32)

    def first(b, state):
        rel = rel_ref[at(b, steps), :]
        k = short_of(x_s, tap, steps, 1, b, rel)
        v = short_of(x_s, tap, steps, 2, b, rel)
        drive = k * v
        k_s[line(b), :] = k
        v_s[line(b), :] = v
        drive_s[line(b), :] = drive
        return tuple(jnp.where(rel >= 1, decay[m] * state[m], 0.0) + drive for m in range(2))

    ends = lax.fori_loop(0, steps, first, (zero, zero), unroll=2)
    joined = rel_ref[at(steps - 1, steps), :] >= steps
    for m in range(2):
        link = jnp.where(joined, whole[m], 0.0)
        carry = jnp.zeros((1, LANES), f32)
        for a in range(SEGS):
            carry_s[m, a : a + 1, :] = carry
            carry = link[a : a + 1, :] * carry + ends[m][a : a + 1, :]

    def second(b, state):
        rel = rel_ref[at(b, steps), :]
        drive = drive_s[line(b), :]
        state = tuple(jnp.where(rel >= 1, decay[m] * state[m], 0.0) + drive for m in range(2))
        filtered = gain[0] * state[0] + gain[1] * state[1] + skip * drive
        filtered_s[line(b), :] = filtered
        for m in range(2):
            state_s[m, line(b), :] = state[m]
        gated_s[pl.ds(b, SEGS, stride=steps), :] = short_of(x_s, tap, steps, 0, b, rel) * filtered
        return state

    lax.fori_loop(0, steps, second, (carry_s[0], carry_s[1]), unroll=2)
    gated_ref[...] = gated_s[0:tokens, :].astype(jnp.bfloat16)


def backward_kernel(
    dg_ref, x_s, k_s, v_s, drive_s, filtered_s, state_s,
    src_row_ref, rel_ref, taps_ref, memory_ref, residue_ref, skip_ref,
    d_fields_ref,
    ds_s, dg_s, df_s, dp_s, carry_s, sums_s,
):
    tokens = dg_ref.shape[0]
    peers = d_fields_ref.shape[0]
    share = tokens // peers
    steps = tokens // SEGS
    block = 256
    f32 = jnp.float32
    for f in range(3):
        ds_s[f, PAD + tokens : PAD + tokens + PAD, :] = jnp.zeros((PAD, LANES), f32)
    dg_s[0:tokens, :] = dg_ref[...].astype(f32)
    decay, norm, gain, whole = modes_of(memory_ref, residue_ref, steps)
    skip = skip_ref[0:1, :]
    tap = taps_of(taps_ref)
    zero = jnp.zeros((SEGS, LANES), f32)

    def third(i, held):
        b = steps - 1 - i
        query = short_of(x_s, tap, steps, 0, b, rel_ref[at(b, steps), :])
        dg = dg_s[pl.ds(b, SEGS, stride=steps), :]
        ds_s[0, at(b, steps), :] = dg * filtered_s[line(b), :]
        df = dg * query
        df_s[line(b), :] = df
        ahead = rel_ref[at(b, steps, 1), :] >= 1
        adjoint = [gain[m] * df + jnp.where(ahead, decay[m] * held[m], 0.0) for m in range(2)]
        sums = [held[2 + m] + df * state_s[m, line(b), :] for m in range(2)]
        return (*adjoint, *sums, held[4] + df * drive_s[line(b), :])

    held = lax.fori_loop(0, steps, third, (zero,) * 5, unroll=2)
    starts = held[:2]
    joined = rel_ref[at(0, steps, steps), :] >= steps
    for m in range(2):
        link = jnp.where(joined, whole[m], 0.0)
        carry = jnp.zeros((1, LANES), f32)
        for a in reversed(range(SEGS)):
            carry_s[m, a : a + 1, :] = carry
            carry = link[a : a + 1, :] * carry + starts[m][a : a + 1, :]

    def fourth(i, adjoint):
        b = steps - 1 - i
        ahead = rel_ref[at(b, steps, 1), :] >= 1
        df = df_s[line(b), :]
        adjoint = tuple(
            gain[m] * df + jnp.where(ahead, decay[m] * adjoint[m], 0.0) for m in range(2)
        )
        d_drive = skip * df + adjoint[0] + adjoint[1]
        ds_s[1, at(b, steps), :] = d_drive * v_s[line(b), :]
        ds_s[2, at(b, steps), :] = d_drive * k_s[line(b), :]
        return adjoint

    lax.fori_loop(0, steps, fourth, (carry_s[0], carry_s[1]), unroll=2)

    def fold(value):
        return jnp.sum(value.reshape(SEGS // 8, 8, LANES), axis=0)

    def fifth(b, sums):
        sums = list(sums)
        rel = [rel_ref[at(b, steps, j), :] for j in range(3)]
        for f in range(3):
            here = ds_s[f, at(b, steps), :]
            d_packed = tap[f][0] * here
            sums[3 * f] = sums[3 * f] + fold(here * x_s[f, at(b, steps), :])
            for j in (1, 2):
                d_packed = d_packed + jnp.where(rel[j] >= j, tap[f][j] * ds_s[f, at(b, steps, j), :], 0.0)
                term = jnp.where(rel[0] >= j, here * x_s[f, at(b, steps, -j), :], 0.0)
                sums[3 * f + j] = sums[3 * f + j] + fold(term)
            dp_s[line(b), f * LANES : (f + 1) * LANES] = d_packed.astype(jnp.bfloat16)
        return tuple(sums)

    none = jnp.zeros((8, LANES), f32)
    sums = lax.fori_loop(0, steps, fifth, (none,) * 9)
    for n in range(9):
        sums_s[n : n + 1, :] = jnp.sum(sums[n], axis=0, keepdims=True)
    for m in range(2):
        sums_s[9 + m : 10 + m, :] = norm[m] * jnp.sum(held[2 + m], axis=0, keepdims=True)
    sums_s[11:12, :] = jnp.sum(held[4], axis=0, keepdims=True)
    sums_s[12:16, :] = jnp.zeros((4, LANES), f32)
    rest = sums_s[...]
    for f in range(3):
        part = rest.astype(jnp.bfloat16)
        rest = rest - part.astype(f32)
        for d in range(peers):
            d_fields_ref[d, share : share + EXTRA, f * LANES : (f + 1) * LANES] = part

    def scatter(i, unused):
        start = pl.multiple_of(i * block, block)
        rows = lax.broadcasted_iota(jnp.int32, (block, tokens), 0) + start
        pick = jnp.where(src_row_ref[...] == rows, 1.0, 0.0).astype(jnp.bfloat16)
        got = jnp.dot(pick, dp_s[...], preferred_element_type=f32)
        d_fields_ref[i // (share // block), pl.ds(start % share, block), :] = got.astype(jnp.bfloat16)
        return unused

    lax.fori_loop(0, tokens // block, scatter, 0)


def plan(tokens):
    steps = tokens // SEGS
    padded = tokens + 2 * PAD + steps
    return steps, padded


def forward_part(x, source, rel, taps, memory, residue, skip, tokens, share):
    steps, padded = plan(tokens)
    f32 = jnp.float32
    column = jax.ShapeDtypeStruct((tokens, LANES), f32)
    return pl.pallas_call(
        forward_kernel,
        out_shape=(
            jax.ShapeDtypeStruct((tokens, LANES), jnp.bfloat16),
            jax.ShapeDtypeStruct((3, padded, LANES), f32),
            column,
            column,
            column,
            column,
            jax.ShapeDtypeStruct((2, tokens, LANES), f32),
        ),
        scratch_shapes=[
            pltpu.VMEM((tokens + steps, LANES), f32),
            pltpu.VMEM((2, SEGS, LANES), f32),
        ],
        compiler_params=pltpu.CompilerParams(vmem_limit_bytes=32 * 1024 * 1024),
        cost_estimate=pl.CostEstimate(flops=20_000_000_000, bytes_accessed=16_000_000, transcendentals=0),
        name="forward_part",
    )(x, (source + EXTRA * (source // share))[:, None], rel, taps, memory, residue, skip)


def backward_part(dg, kept, source, rel, taps, memory, residue, skip, peers):
    tokens = dg.shape[0]
    steps, padded = plan(tokens)
    f32 = jnp.float32
    source_row = source.reshape(SEGS, steps).T.reshape(1, tokens)
    return pl.pallas_call(
        backward_kernel,
        out_shape=jax.ShapeDtypeStruct((peers, tokens // peers + EXTRA, 3 * LANES), jnp.bfloat16),
        scratch_shapes=[
            pltpu.VMEM((3, padded, LANES), f32),
            pltpu.VMEM((tokens + steps, LANES), f32),
            pltpu.VMEM((tokens, LANES), f32),
            pltpu.VMEM((tokens, 3 * LANES), jnp.bfloat16),
            pltpu.VMEM((2, SEGS, LANES), f32),
            pltpu.VMEM((EXTRA, LANES), f32),
        ],
        compiler_params=pltpu.CompilerParams(vmem_limit_bytes=32 * 1024 * 1024),
        cost_estimate=pl.CostEstimate(flops=20_000_000_000, bytes_accessed=16_000_000, transcendentals=0),
        name="backward_part",
    )(dg, *kept, source_row, rel, taps, memory, residue, skip)


def by_channels(
    fields_in, pack_source, doc_start, short_filter, memory, residue, skip_gain, w_out, cotangent
):
    rows, _, width = fields_in.shape
    peers = lax.axis_size("seq")
    here = lax.axis_index("seq")
    tokens = rows * peers
    part = width // peers

    def exchange(shard):
        return lax.all_to_all(shard, "seq", split_axis=0, concat_axis=0, tiled=True)

    fields = fields_in.reshape(rows, 3, peers, part).transpose(2, 0, 1, 3)
    ints = jnp.concatenate([pack_source, doc_start])
    digits = jnp.concatenate([ints // 128, ints % 128]).astype(jnp.bfloat16)
    digits = jnp.pad(digits, (0, EXTRA * 3 * part - digits.shape[0])).reshape(1, EXTRA, 3 * part)
    digits = jnp.broadcast_to(digits, (peers, EXTRA, 3 * part))
    x = exchange(jnp.concatenate([fields.reshape(peers, rows, 3 * part), digits], axis=1))
    digits = x[:, rows:].reshape(peers, EXTRA * 3 * part)[:, : 4 * rows].astype(jnp.int32)
    ints = digits[:, : 2 * rows] * 128 + digits[:, 2 * rows :]
    x = x.reshape(-1, 3 * part)
    d_gated = lax.dot_general(
        lax.all_gather(cotangent, "mp", axis=1, tiled=True),
        w_out,
        (((1,), (1,)), ((), ())),
        preferred_element_type=jnp.float32,
    ).astype(jnp.bfloat16)
    d_gated = d_gated.reshape(rows, peers, part).transpose(1, 0, 2)

    def own(array):
        return lax.dynamic_slice_in_dim(array, here * part, part, array.ndim - 1)

    source = ints[:, :rows].reshape(tokens)
    steps, padded = plan(tokens)
    rel = jnp.arange(tokens, dtype=jnp.int32) - ints[:, rows:].reshape(tokens)
    rel = jnp.broadcast_to(jnp.pad(rel, (PAD, PAD + steps))[:, None], (padded, LANES))
    weights = (
        own(short_filter).reshape(9, part),
        own(memory),
        own(residue),
        own(skip_gain).reshape(1, part),
    )
    gated, *kept = forward_part(x, source, rel, *weights, tokens, rows)
    both = exchange(jnp.concatenate([d_gated, gated.reshape(peers, rows, part)], axis=1))
    dg = both[:, :rows].reshape(tokens, part)
    d_fields = backward_part(dg, kept, source, rel, *weights, peers)
    gated = both[:, rows:].transpose(1, 0, 2).reshape(rows, width)
    arrived = exchange(d_fields)
    d_fields = arrived[:, :rows].reshape(peers, rows, 3, part).transpose(1, 2, 0, 3).reshape(rows, 3, width)
    partial_out = jnp.dot(gated, w_out, preferred_element_type=jnp.float32)
    mixed = lax.psum_scatter(partial_out, "mp", scatter_dimension=1, tiled=True).astype(
        jnp.bfloat16
    )
    sums = arrived[:, rows:].reshape(peers, EXTRA, 3, part).astype(jnp.float32).sum(axis=2)
    sums = sums.transpose(1, 0, 2).reshape(EXTRA, width)
    return (mixed, d_fields, sums[:9].reshape(3, 3, width), sums[9:11], sums[11])


def chosen(*arrays):
    rows, _, width = arrays[0].shape
    peers = lax.axis_size("seq")
    if width == LANES * peers and rows * peers <= 4096 and rows % 256 == 0 and 4 * rows <= EXTRA * 3 * LANES:
        return by_channels(*arrays)
    return per_device(*arrays)


def solution(mesh):
    placed = (
        P("seq", None, "mp"),
        P("seq"),
        P("seq"),
        P(None, None, "mp"),
        P(None, "mp"),
        P(None, "mp"),
        P("mp"),
        P("mp", None),
        P("seq", "mp"),
    )
    return jax.shard_map(
        chosen,
        mesh=mesh,
        in_specs=placed,
        out_specs=(
            P("seq", "mp"),
            P("seq", None, "mp"),
            P(None, None, "mp"),
            P(None, "mp"),
            P("mp"),
        ),
        check_vma=False,
    )
```

```python
import jax
import jax.numpy as jnp
from jax import lax
from jax.experimental import pallas as pl
from jax.experimental.pallas import tpu as pltpu
from jax.sharding import PartitionSpec as P


def shifted(shard, axis, by):
    peers = lax.axis_size(axis)
    pairs = [(i, i + by) for i in range(peers) if 0 <= i + by < peers]
    return lax.ppermute(shard, axis, pairs)


def compose(earlier, later):
    return (earlier[0] * later[0], later[0] * earlier[1] + later[1])


def forward_scan(links, source, axis):
    return lax.associative_scan(compose, (links, source), axis=axis)


def backward_scan(links, source, axis):
    length = links.shape[axis]
    ahead = jnp.concatenate(
        [
            lax.slice_in_dim(links, 1, length, axis=axis),
            jnp.ones_like(lax.slice_in_dim(links, 0, 1, axis=axis)),
        ],
        axis=axis,
    )
    flipped = forward_scan(jnp.flip(ahead, axis), jnp.flip(source, axis), axis)
    return (jnp.flip(flipped[0], axis), jnp.flip(flipped[1], axis))


def rows_of(array, chosen_rows):
    flat = array.reshape(array.shape[0], -1)
    picked = jnp.dot(chosen_rows.astype(array.dtype), flat, preferred_element_type=jnp.float32)
    return picked.astype(array.dtype).reshape((-1,) + array.shape[1:])


def per_device(
    fields_in, pack_source, doc_start, short_filter, memory, residue, skip_gain, w_out, cotangent
):
    rows = fields_in.shape[0]
    width = fields_in.shape[2]
    devices_seq = lax.axis_size("seq")
    here = lax.axis_index("seq")
    capacity = 2 * rows // devices_seq
    source_dev = pack_source // rows
    source_row = pack_source % rows
    line = jnp.arange(rows, dtype=jnp.int32)
    before = (line[:, None] > line[None, :]) & (source_dev[:, None] == source_dev[None, :])
    slot = source_dev * capacity + jnp.sum(before.astype(jnp.int32), axis=1)
    filled = jnp.arange(devices_seq * capacity, dtype=jnp.int32)[:, None] == slot[None, :]
    wanted = jnp.min(jnp.where(filled, source_row[None, :], rows), axis=1)
    wanted = wanted.reshape(devices_seq, capacity)
    asked = lax.all_to_all(wanted, "seq", split_axis=0, concat_axis=0, tiled=True)
    picked = rows_of(fields_in, asked.reshape(-1)[:, None] == line[None, :]).reshape(
        asked.shape[0], asked.shape[1], 3, width
    )
    returned_rows = lax.all_to_all(picked, "seq", split_axis=0, concat_axis=0, tiled=True)
    packed = rows_of(returned_rows.reshape(devices_seq * capacity, 3, width), filled.T)
    position = here * rows + line
    masks = [(position - lag >= doc_start).astype(jnp.float32)[:, None, None] for lag in range(3)]
    tail = shifted(packed[rows - 2 :], "seq", 1)
    extended = jnp.concatenate([tail, packed], axis=0).astype(jnp.float32)
    lagged = [extended[2 - lag : 2 - lag + rows] for lag in range(3)]
    short = masks[0] * short_filter[None, :, 0, :] * lagged[0]
    for lag in (1, 2):
        short = short + masks[lag] * short_filter[None, :, lag, :] * lagged[lag]
    query = short[:, 0]
    keys_part = short[:, 1]
    values_part = short[:, 2]
    drive = keys_part * values_part
    decay = jnp.exp(-1.0 / memory)
    norm_gain = jnp.sqrt(1.0 - decay * decay)
    mode_gain = residue * norm_gain
    part_width = width // devices_seq
    bounds = lax.all_gather(doc_start, "seq", axis=0, tiled=True)
    everywhere = jnp.arange(bounds.shape[0], dtype=jnp.int32)
    link_all = (bounds < everywhere).astype(jnp.float32)
    decay_part = lax.dynamic_slice_in_dim(decay, here * part_width, part_width, 1)
    gain_part = lax.dynamic_slice_in_dim(mode_gain, here * part_width, part_width, 1)
    norm_part = lax.dynamic_slice_in_dim(norm_gain, here * part_width, part_width, 1)
    skip_part = lax.dynamic_slice_in_dim(skip_gain, here * part_width, part_width, 0)
    drive_part = lax.all_to_all(drive.T, "seq", split_axis=0, concat_axis=1, tiled=True)
    links_part = decay_part[:, :, None] * link_all[None, None, :]
    state_part = forward_scan(links_part, jnp.broadcast_to(drive_part[None], links_part.shape), 2)[
        1
    ]
    filtered_part = (
        jnp.sum(gain_part[:, :, None] * state_part, axis=0) + skip_part[:, None] * drive_part
    )
    filtered = lax.all_to_all(filtered_part, "seq", split_axis=1, concat_axis=0, tiled=True).T
    gated = (query * filtered).astype(jnp.bfloat16)
    partial_out = jnp.dot(gated, w_out, preferred_element_type=jnp.float32)
    mixed = lax.psum_scatter(partial_out, "mp", scatter_dimension=1, tiled=True).astype(
        jnp.bfloat16
    )
    d_gated = lax.dot_general(
        lax.all_gather(cotangent, "mp", axis=1, tiled=True),
        w_out,
        (((1,), (1,)), ((), ())),
        preferred_element_type=jnp.float32,
    )
    d_query = d_gated * filtered
    d_filtered = d_gated * query
    grad_part = lax.all_to_all(d_filtered.T, "seq", split_axis=0, concat_axis=1, tiled=True)
    adjoint_part = backward_scan(links_part, gain_part[:, :, None] * grad_part[None], 2)[1]
    back_part = jnp.sum(adjoint_part, axis=0)
    d_drive = (
        skip_gain[None] * d_filtered
        + lax.all_to_all(back_part, "seq", split_axis=1, concat_axis=0, tiled=True).T
    )
    residue_part = norm_part * jnp.sum(grad_part[None] * state_part, axis=2)
    d_residue = lax.all_gather(residue_part, "seq", axis=1, tiled=True)
    d_short = jnp.stack([d_query, d_drive * values_part, d_drive * keys_part], axis=1)
    weighted = [d_short * masks[lag] for lag in range(3)]
    head = jnp.stack(
        [
            short_filter[:, 2, :] * weighted[2][0],
            short_filter[:, 1, :] * weighted[1][0] + short_filter[:, 2, :] * weighted[2][1],
        ],
        axis=0,
    )
    from_next = shifted(head, "seq", -1)
    zero_row = jnp.zeros((1, 3, width), jnp.float32)
    d_packed = short_filter[None, :, 0, :] * weighted[0]
    d_packed = d_packed + short_filter[None, :, 1, :] * jnp.concatenate(
        [weighted[1][1:], zero_row], axis=0
    )
    d_packed = d_packed + short_filter[None, :, 2, :] * jnp.concatenate(
        [weighted[2][2:], zero_row, zero_row], axis=0
    )
    d_packed = d_packed + jnp.concatenate(
        [jnp.zeros((rows - 2, 3, width), jnp.float32), from_next], axis=0
    )
    filter_local = jnp.stack(
        [jnp.sum(weighted[lag] * lagged[lag], axis=0) for lag in range(3)], axis=1
    )
    skip_local = jnp.sum(d_filtered * drive, axis=0)
    d_filter, d_skip = lax.psum((filter_local, skip_local), "seq")
    outgoing = (
        rows_of(d_packed.astype(jnp.bfloat16), filled).reshape(devices_seq, capacity, 3, width)
    )
    returned = lax.all_to_all(outgoing, "seq", split_axis=0, concat_axis=0, tiled=True)
    d_fields = rows_of(returned.reshape(-1, 3, width), line[:, None] == asked.reshape(-1)[None, :])
    return (mixed, d_fields, d_filter, d_residue, d_skip)


EXTRA = 16
PAD = 8
SEGS = 32
LANES = 128


def channel_kernel(
    x_ref, dg_ref, src_col_ref, src_row_ref, rel_ref, taps_ref, memory_ref, residue_ref, skip_ref,
    gated_ref, d_fields_ref,
    x_s, ds_s, dg_s, gated_s, drive_s, k_s, v_s, df_s, dp_s, carry_s, sums_s,
):
    tokens = gated_ref.shape[0]
    peers = d_fields_ref.shape[0]
    share = tokens // peers
    steps = tokens // SEGS
    block = 256
    f32 = jnp.float32
    for f in range(3):
        x_s[f, 0:PAD, :] = jnp.zeros((PAD, LANES), f32)
        ds_s[f, PAD + tokens : PAD + tokens + PAD, :] = jnp.zeros((PAD, LANES), f32)
    dg_s[0:tokens, :] = dg_ref[...].astype(f32)

    def gather(i, unused):
        at = pl.multiple_of(i * block, block)
        rows = lax.broadcasted_iota(jnp.int32, (block, x_ref.shape[0]), 1)
        pick = jnp.where(src_col_ref[pl.ds(at, block), :] == rows, 1.0, 0.0).astype(jnp.bfloat16)
        got = jnp.dot(pick, x_ref[...], preferred_element_type=f32)
        for f in range(3):
            x_s[f, pl.ds(PAD + at, block), :] = got[:, f * LANES : (f + 1) * LANES]
        return unused

    lax.fori_loop(0, tokens // block, gather, 0)

    decay = [jnp.exp(-1.0 / memory_ref[m : m + 1, :]) for m in range(2)]
    norm = [jnp.sqrt(1.0 - d * d) for d in decay]
    gain = [residue_ref[m : m + 1, :] * norm[m] for m in range(2)]
    whole = [jnp.exp(-float(steps) / memory_ref[m : m + 1, :]) for m in range(2)]
    skip = skip_ref[0:1, :]
    tap = [[taps_ref[3 * f + j : 3 * f + j + 1, :] for j in range(3)] for f in range(3)]

    def at(b, shift=0):
        return pl.ds(PAD + b + shift, SEGS, stride=steps)

    def line(b):
        return pl.ds(pl.multiple_of(b * SEGS, SEGS), SEGS)

    def short(f, b, rel):
        total = tap[f][0] * x_s[f, at(b), :]
        for j in (1, 2):
            total = total + jnp.where(rel >= j, tap[f][j] * x_s[f, at(b, -j), :], 0.0)
        return total

    zero = jnp.zeros((SEGS, LANES), f32)

    def first(b, state):
        rel = rel_ref[at(b), :]
        k = short(1, b, rel)
        v = short(2, b, rel)
        drive = k * v
        k_s[line(b), :] = k
        v_s[line(b), :] = v
        drive_s[line(b), :] = drive
        return tuple(jnp.where(rel >= 1, decay[m] * state[m], 0.0) + drive for m in range(2))

    ends = lax.fori_loop(0, steps, first, (zero, zero), unroll=4)
    joined = rel_ref[at(steps - 1), :] >= steps
    for m in range(2):
        link = jnp.where(joined, whole[m], 0.0)
        carry = jnp.zeros((1, LANES), f32)
        for a in range(SEGS):
            carry_s[m, a : a + 1, :] = carry
            carry = link[a : a + 1, :] * carry + ends[m][a : a + 1, :]

    def second(b, held):
        s0, s1, r0, r1, r2 = held
        rel = rel_ref[at(b), :]
        drive = drive_s[line(b), :]
        s0 = jnp.where(rel >= 1, decay[0] * s0, 0.0) + drive
        s1 = jnp.where(rel >= 1, decay[1] * s1, 0.0) + drive
        filtered = gain[0] * s0 + gain[1] * s1 + skip * drive
        query = short(0, b, rel)
        gated_s[pl.ds(b, SEGS, stride=steps), :] = query * filtered
        dg = dg_s[pl.ds(b, SEGS, stride=steps), :]
        ds_s[0, at(b), :] = dg * filtered
        df = dg * query
        df_s[line(b), :] = df
        return (s0, s1, r0 + df * s0, r1 + df * s1, r2 + df * drive)

    held = (carry_s[0], carry_s[1], zero, zero, zero)
    held = lax.fori_loop(0, steps, second, held, unroll=4)
    gated_ref[...] = gated_s[0:tokens, :].astype(jnp.bfloat16)

    def third(i, adjoint):
        b = steps - 1 - i
        ahead = rel_ref[at(b, 1), :] >= 1
        df = df_s[line(b), :]
        return tuple(gain[m] * df + jnp.where(ahead, decay[m] * adjoint[m], 0.0) for m in range(2))

    starts = lax.fori_loop(0, steps, third, (zero, zero), unroll=4)
    joined = rel_ref[at(0, steps), :] >= steps
    for m in range(2):
        link = jnp.where(joined, whole[m], 0.0)
        carry = jnp.zeros((1, LANES), f32)
        for a in reversed(range(SEGS)):
            carry_s[m, a : a + 1, :] = carry
            carry = link[a : a + 1, :] * carry + starts[m][a : a + 1, :]

    def fourth(i, adjoint):
        b = steps - 1 - i
        ahead = rel_ref[at(b, 1), :] >= 1
        df = df_s[line(b), :]
        adjoint = tuple(
            gain[m] * df + jnp.where(ahead, decay[m] * adjoint[m], 0.0) for m in range(2)
        )
        d_drive = skip * df + adjoint[0] + adjoint[1]
        ds_s[1, at(b), :] = d_drive * v_s[line(b), :]
        ds_s[2, at(b), :] = d_drive * k_s[line(b), :]
        return adjoint

    lax.fori_loop(0, steps, fourth, (carry_s[0], carry_s[1]), unroll=4)

    def fold(value):
        return jnp.sum(value.reshape(SEGS // 8, 8, LANES), axis=0)

    def fifth(b, sums):
        sums = list(sums)
        rel = [rel_ref[at(b, j), :] for j in range(3)]
        for f in range(3):
            here = ds_s[f, at(b), :]
            d_packed = tap[f][0] * here
            sums[3 * f] = sums[3 * f] + fold(here * x_s[f, at(b), :])
            for j in (1, 2):
                d_packed = d_packed + jnp.where(rel[j] >= j, tap[f][j] * ds_s[f, at(b, j), :], 0.0)
                term = jnp.where(rel[0] >= j, here * x_s[f, at(b, -j), :], 0.0)
                sums[3 * f + j] = sums[3 * f + j] + fold(term)
            dp_s[line(b), f * LANES : (f + 1) * LANES] = d_packed.astype(jnp.bfloat16)
        return tuple(sums)

    none = jnp.zeros((8, LANES), f32)
    sums = lax.fori_loop(0, steps, fifth, (none,) * 9, unroll=2)
    for n in range(9):
        sums_s[n : n + 1, :] = jnp.sum(sums[n], axis=0, keepdims=True)
    for m in range(2):
        sums_s[9 + m : 10 + m, :] = norm[m] * jnp.sum(held[2 + m], axis=0, keepdims=True)
    sums_s[11:12, :] = jnp.sum(held[4], axis=0, keepdims=True)
    sums_s[12:16, :] = jnp.zeros((4, LANES), f32)
    rest = sums_s[...]
    for f in range(3):
        part = rest.astype(jnp.bfloat16)
        rest = rest - part.astype(f32)
        for d in range(peers):
            d_fields_ref[d, share : share + EXTRA, f * LANES : (f + 1) * LANES] = part

    def scatter(i, unused):
        start = pl.multiple_of(i * block, block)
        rows = lax.broadcasted_iota(jnp.int32, (block, tokens), 0) + start
        pick = jnp.where(src_row_ref[...] == rows, 1.0, 0.0).astype(jnp.bfloat16)
        got = jnp.dot(pick, dp_s[...], preferred_element_type=f32)
        d_fields_ref[i // (share // block), pl.ds(start % share, block), :] = got.astype(jnp.bfloat16)
        return unused

    lax.fori_loop(0, tokens // block, scatter, 0)


def channel_part(x, dg, source, starts, taps, memory, residue, skip, peers):
    tokens = dg.shape[0]
    share = tokens // peers
    steps = tokens // SEGS
    rel = jnp.arange(tokens, dtype=jnp.int32) - starts
    rel = jnp.broadcast_to(jnp.pad(rel, (PAD, PAD + steps))[:, None], (tokens + 2 * PAD + steps, LANES))
    source_row = source.reshape(SEGS, steps).T.reshape(1, tokens)
    f32 = jnp.float32
    padded = tokens + 2 * PAD + steps
    return pl.pallas_call(
        channel_kernel,
        out_shape=(
            jax.ShapeDtypeStruct((tokens, LANES), jnp.bfloat16),
            jax.ShapeDtypeStruct((peers, share + EXTRA, 3 * LANES), jnp.bfloat16),
        ),
        scratch_shapes=[
            pltpu.VMEM((3, padded, LANES), f32),
            pltpu.VMEM((3, padded, LANES), f32),
            pltpu.VMEM((tokens + steps, LANES), f32),
            pltpu.VMEM((tokens + steps, LANES), f32),
            pltpu.VMEM((tokens, LANES), f32),
            pltpu.VMEM((tokens, LANES), f32),
            pltpu.VMEM((tokens, LANES), f32),
            pltpu.VMEM((tokens, LANES), f32),
            pltpu.VMEM((tokens, 3 * LANES), jnp.bfloat16),
            pltpu.VMEM((2, SEGS, LANES), f32),
            pltpu.VMEM((EXTRA, LANES), f32),
        ],
        compiler_params=pltpu.CompilerParams(vmem_limit_bytes=48 * 1024 * 1024),
        name="channel_part",
    )(x, dg, (source + EXTRA * (source // share))[:, None], source_row, rel, taps, memory, residue, skip)


def by_channels(
    fields_in, pack_source, doc_start, short_filter, memory, residue, skip_gain, w_out, cotangent
):
    rows, _, width = fields_in.shape
    peers = lax.axis_size("seq")
    here = lax.axis_index("seq")
    tokens = rows * peers
    part = width // peers

    def exchange(shard):
        return lax.all_to_all(shard, "seq", split_axis=0, concat_axis=0, tiled=True)

    fields = fields_in.reshape(rows, 3, peers, part).transpose(2, 0, 1, 3)
    ints = jnp.concatenate([pack_source, doc_start])
    digits = jnp.concatenate([ints // 128, ints % 128]).astype(jnp.bfloat16)
    digits = jnp.pad(digits, (0, EXTRA * 3 * part - digits.shape[0])).reshape(1, EXTRA, 3 * part)
    digits = jnp.broadcast_to(digits, (peers, EXTRA, 3 * part))
    x = exchange(jnp.concatenate([fields.reshape(peers, rows, 3 * part), digits], axis=1))
    digits = x[:, rows:].reshape(peers, EXTRA * 3 * part)[:, : 4 * rows].astype(jnp.int32)
    ints = digits[:, : 2 * rows] * 128 + digits[:, 2 * rows :]
    x = x.reshape(-1, 3 * part)
    d_gated = lax.dot_general(
        lax.all_gather(cotangent, "mp", axis=1, tiled=True),
        w_out,
        (((1,), (1,)), ((), ())),
        preferred_element_type=jnp.float32,
    ).astype(jnp.bfloat16)
    dg = exchange(d_gated.reshape(rows, peers, part).transpose(1, 0, 2)).reshape(tokens, part)

    def own(array):
        return lax.dynamic_slice_in_dim(array, here * part, part, array.ndim - 1)

    gated, d_fields = channel_part(
        x,
        dg,
        ints[:, :rows].reshape(tokens),
        ints[:, rows:].reshape(tokens),
        own(short_filter).reshape(9, part),
        own(memory),
        own(residue),
        own(skip_gain).reshape(1, part),
        peers,
    )
    gated = exchange(gated.reshape(peers, rows, part)).transpose(1, 0, 2).reshape(rows, width)
    arrived = exchange(d_fields)
    d_fields = arrived[:, :rows].reshape(peers, rows, 3, part).transpose(1, 2, 0, 3).reshape(rows, 3, width)
    partial_out = jnp.dot(gated, w_out, preferred_element_type=jnp.float32)
    mixed = lax.psum_scatter(partial_out, "mp", scatter_dimension=1, tiled=True).astype(
        jnp.bfloat16
    )
    sums = arrived[:, rows:].reshape(peers, EXTRA, 3, part).astype(jnp.float32).sum(axis=2)
    sums = sums.transpose(1, 0, 2).reshape(EXTRA, width)
    return (mixed, d_fields, sums[:9].reshape(3, 3, width), sums[9:11], sums[11])


def chosen(*arrays):
    rows, _, width = arrays[0].shape
    peers = lax.axis_size("seq")
    if width == LANES * peers and rows * peers <= 4096 and rows % 256 == 0 and 4 * rows <= EXTRA * 3 * LANES:
        return by_channels(*arrays)
    return per_device(*arrays)


def solution(mesh):
    placed = (
        P("seq", None, "mp"),
        P("seq"),
        P("seq"),
        P(None, None, "mp"),
        P(None, "mp"),
        P(None, "mp"),
        P("mp"),
        P("mp", None),
        P("seq", "mp"),
    )
    return jax.shard_map(
        chosen,
        mesh=mesh,
        in_specs=placed,
        out_specs=(
            P("seq", "mp"),
            P("seq", None, "mp"),
            P(None, None, "mp"),
            P(None, "mp"),
            P("mp"),
        ),
        check_vma=False,
    )
```
